32 devices in a mesh: px: 8 (over y, x, core), py: 4 (over z).
Axes of the slice: x: 2, y: 2, z: 4, core: 2. Of those that a mesh axis runs over, the one named last changes fastest.
Arguments:
- cotangent: float32 [64, 64, 128], P('px', 'py'), may hold values from -6 to 6
- fraction: float32 [3, 64, 64, 128], P(None, 'px', 'py'), may hold values from 0 to 0.999
- grid_base: int32 [3, 64, 64, 128], P(None, 'px', 'py'), may hold values from 0 to 255, as said below
- cell_count: int32 [64, 64], P('px', 'py'), may hold values from 32 to 128, as said below
- influence: float32 [256, 256, 256], P(('px', 'py')), as said below
Outputs:
- charge_gradient: float32 [64, 64, 128], P('px', 'py')
The draws below stay inside these ranges and needn't reach their ends.
Inputs may be any that keep to these rules, and one draw needn't show every extreme that they name: grid_base[0] // 4 is the cell's first index and grid_base[1] // 4 its second; grid_base[2] lies in 0 to 255. `cell_count`: some cell is full. Positive and even: influence[kz, kx, ky] equals influence[-kz, -kx, -ky], wave numbers taken modulo 256, 256, 256.
All inputs are finite; a program needn't handle non-finite values.
Results may differ from the reference program's by a relative error of at most 0.0003.
Values sent between devices are 32-bit elements; how exact they have to be, the bound alone decides.
A program may use at most 128 MiB of HBM per device.

```python
import math
import jax
import jax.numpy as jnp
from jax import lax

NZ = 256
CELL = 4
SLOTS = 128
NX = 256
NY = 256
NCX = 64
NCY = 64


def draw_grid_base(key, part):
    key = jax.random.fold_in(key, 11)
    first_key, second_key, third_key = jax.random.split(key, 3)
    atom_shape = (NCX, NCY, SLOTS)
    start_x = (jnp.arange(NCX, dtype=jnp.int32) * CELL)[:, None, None]
    start_y = (jnp.arange(NCY, dtype=jnp.int32) * CELL)[None, :, None]
    along_x = start_x + jax.random.randint(first_key, atom_shape, 0, CELL, dtype=jnp.int32)
    along_y = start_y + jax.random.randint(second_key, atom_shape, 0, CELL, dtype=jnp.int32)
    along_z = jax.random.randint(third_key, atom_shape, 0, NZ, dtype=jnp.int32)
    along_x = along_x.at[NCX - 1, 0, 0].set(NX - 1).at[0, 0, 1].set(0)
    along_y = along_y.at[0, NCY - 1, 0].set(NY - 1).at[0, 0, 1].set(0)
    along_z = along_z.at[0, 0, 0].set(NZ - 1).at[0, 0, 1].set(0)
    return jnp.stack([along_x, along_y, along_z]).astype(jnp.int32)


def draw_cell_count(key, part):
    key = jax.random.fold_in(key, 23)
    first_key, second_key = jax.random.split(key, 2)
    cells_total = NCX * NCY
    counts = jax.random.randint(first_key, (cells_total,), max(1, SLOTS // 4), SLOTS + 1, dtype=jnp.int32)
    chosen = jax.random.randint(second_key, (), 0, cells_total, dtype=jnp.int32)
    counts = jnp.where(jnp.arange(cells_total, dtype=jnp.int32) == chosen, SLOTS, counts)
    return counts.reshape(NCX, NCY).astype(jnp.int32)


def wave_numbers(length):
    indices = jnp.arange(length, dtype=jnp.int32)
    return jnp.minimum(indices, length - indices).astype(jnp.float32) / length


def draw_influence(key, part):
    key = jax.random.fold_in(key, 37)
    along_z = wave_numbers(NZ)[:, None, None]
    along_x = wave_numbers(NX)[None, :, None]
    along_y = wave_numbers(NY)[None, None, :]
    squared = along_z * along_z + along_x * along_x + along_y * along_y
    envelope = 0.3 / (squared + 1.0 / (NX * NY)) + 10.0
    raw = jax.random.uniform(key, (NZ, NX, NY), jnp.float32, 0.0, 1.0)
    mirror = jnp.roll(jnp.flip(raw, (0, 1, 2)), 1, axis=(0, 1, 2))
    even = 0.5 * (raw + mirror)
    factor = jnp.exp(math.log(0.5) + math.log(4.0) * even)
    return (factor * envelope).astype(jnp.float32)


def steps_of(key, shape, shards, smallest, high):
    level, own = 1.0, jax.random.fold_in(key, 6)
    for dim, blocks in shards:
        steps = jnp.exp(jax.random.uniform(jax.random.fold_in(own, dim), (blocks,), jnp.float32, smallest / len(shards), high / len(shards)))
        level = level * jnp.repeat(steps, shape[dim] // blocks).reshape([-1 if axis == dim else 1 for axis in range(len(shape))])
    return level


def scatter_about(stream_key, shape, width, limit, cuts=(), held_as=jnp.bfloat16):
    values = jax.random.normal(stream_key, shape, jnp.float32) * width
    if len(cuts) > 0:
        values = steps_of(stream_key, shape, cuts, -0.22, 0.18) * values
    return jnp.clip(values, min=-limit, max=limit).astype(held_as)


def setup_inputs(seed: int = 0) -> dict:
    streams_of = jax.random.split(jax.random.key(seed), 6)
    return {
        "cotangent": scatter_about(streams_of[0], (NCX, NCY, SLOTS), 1.0, 6.0, ((0, 8), (1, 4)), jnp.float32),
        "fraction": jnp.clip(0.999 * jax.random.uniform(streams_of[1], (3, NCX, NCY, SLOTS), jnp.float32) ** steps_of(streams_of[1], (3, NCX, NCY, SLOTS), ((1, 8), (2, 4)), -0.2, 0.2), 0.0, 0.999),
        "grid_base": draw_grid_base(jax.random.fold_in(streams_of[5], 71), 0),
        "cell_count": draw_cell_count(jax.random.fold_in(streams_of[5], 71), 0),
        "influence": draw_influence(jax.random.fold_in(streams_of[5], 71), 0),
    }


def spline_weights(fractions):
    nothing = jnp.zeros_like(fractions)
    values = [fractions, 1.0 - fractions]
    for degree in (3, 4, 5):
        updated = []
        for position in range(degree):
            upper_term = values[position] if position < degree - 1 else nothing
            lower_term = values[position - 1] if position >= 1 else nothing
            updated.append(((fractions + position) * upper_term + (degree - fractions - position) * lower_term) / (degree - 1))
        values = updated
    return jnp.stack(values)


def reference(cotangent, fraction, grid_base, cell_count, influence):
    slot_ids = jnp.arange(SLOTS, dtype=jnp.int32)
    occupied = slot_ids[None, None, :] < cell_count[:, :, None]
    charge = jnp.where(occupied, cotangent, jnp.zeros_like(cotangent))
    shifts = 2 - jnp.arange(5, dtype=jnp.int32)
    frac_rows = jnp.moveaxis(fraction, 1, 0)
    base_rows = jnp.moveaxis(grid_base, 1, 0)

    def points(frac_row, base_row):
        index_x = ((base_row[0][None] + shifts[:, None, None]) % NX).astype(jnp.int32)
        index_y = ((base_row[1][None] + shifts[:, None, None]) % NY).astype(jnp.int32)
        index_z = ((base_row[2][None] + shifts[:, None, None]) % NZ).astype(jnp.int32)
        across_x = spline_weights(frac_row[0])[:, None, None]
        across_y = spline_weights(frac_row[1])[None, :, None]
        across_z = spline_weights(frac_row[2])[None, None, :]
        indices = (index_x[:, None, None], index_y[None, :, None], index_z[None, None, :])
        return indices, across_x, across_y, across_z

    def spread_step(mesh_grid, row):
        charge_row, frac_row, base_row = row
        indices, across_x, across_y, across_z = points(frac_row, base_row)
        values = ((charge_row * across_x) * across_y) * across_z
        return mesh_grid.at[indices].add(values), None

    spread, unused = lax.scan(spread_step, jnp.zeros((NX, NY, NZ), jnp.float32), (charge, frac_rows, base_rows))
    spectrum = jnp.fft.fftn(spread)
    scaled = spectrum * jnp.transpose(influence, (1, 2, 0))
    potential = jnp.real(jnp.fft.ifftn(scaled)).astype(jnp.float32)

    def gather_step(carry, row):
        frac_row, base_row = row
        indices, across_x, across_y, across_z = points(frac_row, base_row)
        values = potential[indices] * ((across_x * across_y) * across_z)
        return carry, jnp.sum(values, axis=(0, 1, 2))

    unused_carry, gradient = lax.scan(gather_step, jnp.zeros((), jnp.float32), (frac_rows, base_rows))
    return jnp.where(occupied, gradient, jnp.zeros_like(gradient))
```

```python
import functools
import math

import jax
import jax.numpy as jnp
import ml_dtypes
import numpy as np
from jax import lax
from jax.experimental import pallas as pl
from jax.experimental.pallas import tpu as pltpu
from jax.sharding import PartitionSpec as P

CELL = 4
REACH = 8
VMEM_LIMIT = 48 * 1024 * 1024


def halves_np(table):
    high = np.asarray(table, np.float32).astype(ml_dtypes.bfloat16)
    low = (np.asarray(table, np.float64) - high.astype(np.float64)).astype(ml_dtypes.bfloat16)
    return jnp.asarray(np.stack([high, low]))


def halves(value):
    high = value.astype(jnp.bfloat16)
    low = (value - high.astype(jnp.float32)).astype(jnp.bfloat16)
    return high, low


def dot3(left, right, dims):
    def one(a, b):
        return lax.dot_general(a, b, (dims, ((), ())), preferred_element_type=jnp.float32)

    return one(left[0], right[0]) + (one(left[0], right[1]) + one(left[1], right[0]))


NN = ((1,), (0,))
NT = ((1,), (1,))


def spline_weights(fractions):
    values = [fractions, 1.0 - fractions]
    for degree in (3, 4, 5):
        updated = []
        for position in range(degree):
            term = None
            if position < degree - 1:
                term = (fractions + position) * values[position]
            if position >= 1:
                lower = (degree - fractions - position) * values[position - 1]
                term = lower if term is None else term + lower
            updated.append(term * (1.0 / (degree - 1)))
        values = updated
    return values


def window_weights(offset, weights):
    position = lax.broadcasted_iota(jnp.int32, (REACH, offset.shape[1]), 0)
    selected = 4 + offset - position
    total = jnp.zeros(selected.shape, jnp.float32)
    for degree in range(5):
        total = jnp.where(selected == degree, weights[degree], total)
    return total


def depth_weights(base, weights, size):
    level = lax.broadcasted_iota(jnp.int32, (size, base.shape[1]), 0)
    selected = (base + 2 - level) & (size - 1)
    total = jnp.zeros(selected.shape, jnp.float32)
    for degree in range(5):
        total = jnp.where(selected == degree, weights[degree], total)
    return total


def cell_tables(across, base_ref, cell, size):
    def row(values):
        return [value[cell : cell + 1, :] for value in values]

    window_x = window_weights(base_ref[0, 0, cell : cell + 1, :] & (CELL - 1), row(across[0]))
    window_y = window_weights(base_ref[1, 0, cell : cell + 1, :] & (CELL - 1), row(across[1]))
    depth = depth_weights(base_ref[2, 0, cell : cell + 1, :], row(across[2]), size)
    return window_x, window_y, halves(depth)


def spread_kernel(size, charge_ref, fraction_ref, base_ref, out_ref):
    row = pl.program_id(0)

    @pl.when(row == 0)
    def _():
        out_ref[...] = jnp.zeros_like(out_ref)

    across = [spline_weights(fraction_ref[dim, 0]) for dim in range(3)]
    charge = charge_ref[0]
    cells_y, slots = charge.shape
    for cell in range(cells_y):
        window_x, window_y, depth = cell_tables(across, base_ref, cell, size)
        loaded = charge[cell : cell + 1, :] * window_x
        lifted = (loaded[:, None, :] * window_y[None, :, :]).reshape(REACH * REACH, slots)
        patch = dot3(halves(lifted), depth, NT).reshape(REACH, REACH, size)
        span = (pl.ds(row * CELL, REACH), pl.ds(cell * CELL, REACH), slice(None))
        out_ref[span] = out_ref[span] + patch


def gather_kernel(size, fraction_ref, base_ref, grid_ref, out_ref):
    row = pl.program_id(0)
    across = [spline_weights(fraction_ref[dim, 0]) for dim in range(3)]
    cells_y, slots = fraction_ref.shape[2:]
    for cell in range(cells_y):
        window_x, window_y, depth = cell_tables(across, base_ref, cell, size)
        span = (pl.ds(row * CELL, REACH), pl.ds(cell * CELL, REACH), slice(None))
        window = grid_ref[span].reshape(REACH * REACH, size)
        value = dot3(halves(window), depth, NN).reshape(REACH, REACH, slots)
        value = jnp.sum(value * window_x[:, None, :], axis=0) * window_y
        out_ref[0, cell : cell + 1, :] = jnp.sum(value, axis=0, keepdims=True)


def depth_forward_kernel(grid_ref, table_ref, out_ref):
    extent_x, extent_y, size = grid_ref.shape
    pairs = extent_x // 2
    table = (table_ref[0], table_ref[1])
    for pair in range(pairs):
        block = grid_ref[2 * pair : 2 * pair + 2].reshape(2 * extent_y, size)
        out_ref[pl.ds(pair, size, stride=pairs), :] = dot3(table, halves(block), NT)


def depth_inverse_kernel(in_ref, table_ref, out_ref):
    extent_x, extent_y, size = out_ref.shape
    pairs = extent_x // 2
    table = (table_ref[0], table_ref[1])
    for pair in range(pairs):
        block = in_ref[pl.ds(pair, size, stride=pairs), :].T
        out_ref[2 * pair : 2 * pair + 2] = dot3(halves(block), table, NN).reshape(
            2, extent_y, size
        )


def plane_kernel(
    start_ref, in_ref, own_ref, other_ref, right_ref, back_ref, left_ref, left_back_ref, out_ref
):
    count_x, count_y, parts, pairs, lanes = in_ref.shape
    half = lanes // 2
    rows = count_x * pairs
    full_y = count_y * half
    full_x = 2 * rows
    right = (right_ref[0], right_ref[1])
    back = (back_ref[0], back_ref[1])
    left = (left_ref[0], left_ref[1])
    left_back = (left_back_ref[0], left_back_ref[1])

    def load(part):
        blocks = [in_ref[:, y, part].reshape(rows, lanes) for y in range(count_y)]
        top = jnp.concatenate([block[:, :half] for block in blocks], axis=1)
        bottom = jnp.concatenate([block[:, half:] for block in blocks], axis=1)
        return jnp.concatenate([top, bottom], axis=0)

    def along_x(table, real, imag):
        both = dot3(table, halves(jnp.concatenate([real, imag], axis=1)), NN)
        upper, lower = both[:full_x], both[full_x:]
        return (
            upper[:, :full_y] - lower[:, full_y:],
            upper[:, full_y:] + lower[:, :full_y],
        )

    first = dot3(halves(load(0)), right, NN)
    second = dot3(halves(load(1)), right, NN)
    first = (first[:, :full_y], first[:, full_y:])
    second = (second[:, :full_y], second[:, full_y:])

    def finish(real, imag):
        real, imag = along_x(left_back, real, imag)
        both = dot3(halves(jnp.concatenate([real, imag], axis=0)), back, NN)
        upper, lower = both[:full_x], both[full_x:]
        results = (
            upper[:, :full_y] - lower[:, full_y:],
            upper[:, full_y:] + lower[:, :full_y],
        )
        for part in range(2):
            result = results[part]
            for y in range(count_y):
                columns = slice(y * half, (y + 1) * half)
                block = jnp.concatenate(
                    [result[:rows, columns], result[rows:, columns]], axis=1
                )
                out_ref[:, y, part] = block.reshape(count_x, pairs, lanes)

    own = own_ref[0]

    @pl.when(pl.program_id(0) == 0)
    def _():
        other = other_ref[0]
        ar, ai = along_x(left, *first)
        br, bi = along_x(left, *second)
        finish(own * ar - other * bi, own * ai + other * br)

    @pl.when(pl.program_id(0) != 0)
    def _():
        real, imag = along_x(left, first[0] - second[1], first[1] + second[0])
        finish(own * real, own * imag)


def with_halo(block, sides, width):
    for axis, dim in sides:
        count = lax.axis_size(axis)
        forward = [(i, (i + 1) % count) for i in range(count)]
        backward = [(target, source) for source, target in forward]
        low = lax.ppermute(
            lax.slice_in_dim(block, block.shape[dim] - width, None, axis=dim), axis, forward
        )
        high = lax.ppermute(lax.slice_in_dim(block, 0, width, axis=dim), axis, backward)
        block = jnp.concatenate([low, block, high], axis=dim)
    return block


def fold_halo(block, sides, width):
    for axis, dim in sides:
        count = lax.axis_size(axis)
        extent = block.shape[dim]
        forward = [(i, (i + 1) % count) for i in range(count)]
        backward = [(target, source) for source, target in forward]
        low = lax.ppermute(
            lax.slice_in_dim(block, extent - width, None, axis=dim), axis, forward
        )
        high = lax.ppermute(lax.slice_in_dim(block, 0, width, axis=dim), axis, backward)

        def part(start, stop):
            return lax.slice_in_dim(block, start, stop, axis=dim)

        block = jnp.concatenate(
            [
                part(width, 2 * width) + low,
                part(2 * width, extent - 2 * width),
                part(extent - 2 * width, extent - width) + high,
            ],
            axis=dim,
        )
    return block


def wave_tables(size, devices, scale):
    each = size // devices
    rows, weights = [], []
    points = np.arange(size)
    for device in range(devices):
        for plane in range(each // 2):
            wave = device * each + plane + (0 if device < devices // 2 else 1)
            angle = (wave * points % size) * (2.0 * math.pi / size)
            if wave == 0:
                rows += [np.ones(size), 1.0 - 2.0 * (points % 2)]
                weights += [1.0, 1.0]
            else:
                rows += [np.cos(angle), -np.sin(angle)]
                weights += [2.0, 2.0]
    forward = np.stack(rows)
    return forward, forward * (np.array(weights)[:, None] * scale)


def angles(first, second, size):
    return (first[:, None] * second[None, :] % size) * (2.0 * math.pi / size)


def per_device(cotangent, fraction, grid_base, cell_count, influence):
    cells_x, cells_y, slots = cotangent.shape
    full_x, full_y = influence.shape[1:]
    px_size = lax.axis_size("px")
    py_size = lax.axis_size("py")
    devices = px_size * py_size
    each = influence.shape[0]
    size = each * devices
    planes = each // 2
    local_x = cells_x * CELL
    local_y = cells_y * CELL
    pairs = local_x // 2
    lanes = 2 * local_y
    params = pltpu.CompilerParams(vmem_limit_bytes=VMEM_LIMIT)
    device = lax.axis_index("px") * py_size + lax.axis_index("py")

    occupied = jnp.arange(slots, dtype=jnp.int32)[None, None, :] < cell_count[:, :, None]
    charge = jnp.where(occupied, cotangent, 0.0)

    extra = lax.ppermute(influence[:1], ("px", "py"), [(devices // 2, 0)])
    start = jnp.where(device < devices // 2, 0, 1).astype(jnp.int32)
    own_first = lax.dynamic_slice_in_dim(influence, start, 1, axis=0)
    other = jnp.where(device == 0, extra, own_first)

    whole = lambda *dims: pl.BlockSpec(dims, lambda *_: (0,) * len(dims))
    atoms = pl.BlockSpec((3, 1, cells_y, slots), lambda i: (0, i, 0, 0))
    cells = pl.BlockSpec((1, cells_y, slots), lambda i: (i, 0, 0))

    extended = pl.pallas_call(
        functools.partial(spread_kernel, size),
        grid=(cells_x,),
        in_specs=[cells, atoms, atoms],
        out_specs=whole(local_x + 4, local_y + 4, size),
        out_shape=jax.ShapeDtypeStruct((local_x + 4, local_y + 4, size), jnp.float32),
        compiler_params=params,
        name="spread",
    )(charge, fraction, grid_base)
    spread = fold_halo(extended, (("px", 0), ("py", 1)), 2)

    forward_z, inverse_z = wave_tables(size, devices, 1.0 / (size * full_x * full_y))
    columns = pl.pallas_call(
        depth_forward_kernel,
        out_shape=jax.ShapeDtypeStruct((size * pairs, lanes), jnp.float32),
        compiler_params=params,
        name="depth_forward",
    )(spread, halves_np(forward_z))
    mixed = lax.all_to_all(columns, ("px", "py"), split_axis=0, concat_axis=0, tiled=True)
    mixed = mixed.reshape(px_size, py_size, 2 * planes, pairs, lanes)

    order = np.arange(full_x).reshape(full_x // 2, 2).T.reshape(-1)
    y_angles = angles(np.arange(full_y), np.arange(full_y), full_y)
    x_angles = angles(np.arange(full_x), order, full_x)
    right = np.concatenate([np.cos(y_angles), -np.sin(y_angles)], axis=1)
    back = np.concatenate([np.cos(y_angles), np.sin(y_angles)], axis=1)
    left = np.concatenate([np.cos(x_angles), -np.sin(x_angles)], axis=0)
    left_back = np.concatenate([np.cos(x_angles.T), np.sin(x_angles.T)], axis=0)
    block = pl.BlockSpec(
        (px_size, py_size, 2, pairs, lanes), lambda i, start: (0, 0, i, 0, 0)
    )
    turned = pl.pallas_call(
        plane_kernel,
        grid_spec=pltpu.PrefetchScalarGridSpec(
            num_scalar_prefetch=1,
            grid=(planes,),
            in_specs=[
                block,
                pl.BlockSpec((1, full_x, full_y), lambda i, start: (i + start[0], 0, 0)),
                whole(1, full_x, full_y),
                whole(2, full_y, 2 * full_y),
                whole(2, full_y, 2 * full_y),
                whole(2, 2 * full_x, full_x),
                whole(2, 2 * full_x, full_x),
            ],
            out_specs=block,
        ),
        out_shape=jax.ShapeDtypeStruct(mixed.shape, jnp.float32),
        compiler_params=params,
        name="planes",
    )(
        start[None],
        mixed,
        influence,
        other,
        halves_np(right),
        halves_np(back),
        halves_np(left),
        halves_np(left_back),
    )
    returned = lax.all_to_all(
        turned.reshape(size * pairs, lanes), ("px", "py"), split_axis=0, concat_axis=0, tiled=True
    )
    potential = pl.pallas_call(
        depth_inverse_kernel,
        out_shape=jax.ShapeDtypeStruct((local_x, local_y, size), jnp.float32),
        compiler_params=params,
        name="depth_inverse",
    )(returned, halves_np(inverse_z))
    halo_potential = with_halo(potential, (("px", 0), ("py", 1)), 2)
    gradient = pl.pallas_call(
        functools.partial(gather_kernel, size),
        grid=(cells_x,),
        in_specs=[atoms, atoms, whole(local_x + 4, local_y + 4, size)],
        out_specs=cells,
        out_shape=jax.ShapeDtypeStruct(cotangent.shape, jnp.float32),
        compiler_params=params,
        name="gather",
    )(fraction, grid_base, halo_potential)
    return jnp.where(occupied, gradient, 0.0)


def solution(mesh):
    placed = (
        P("px", "py", None),
        P(None, "px", "py", None),
        P(None, "px", "py", None),
        P("px", "py"),
        P(("px", "py"), None, None),
    )
    return jax.shard_map(
        per_device, mesh=mesh, in_specs=placed, out_specs=P("px", "py", None), check_vma=False
    )
```

```python
import functools
import math

import jax
import jax.numpy as jnp
import ml_dtypes
import numpy as np
from jax import lax
from jax.experimental import pallas as pl
from jax.experimental.pallas import tpu as pltpu
from jax.sharding import PartitionSpec as P

CELL = 4
REACH = 8
VMEM_LIMIT = 48 * 1024 * 1024
MESH = pl.DeviceIdType.MESH


def halves_np(table):
    high = np.asarray(table, np.float32).astype(ml_dtypes.bfloat16)
    low = (np.asarray(table, np.float64) - high.astype(np.float64)).astype(ml_dtypes.bfloat16)
    return jnp.asarray(np.stack([high, low]))


def halves(value):
    high = value.astype(jnp.bfloat16)
    low = (value - high.astype(jnp.float32)).astype(jnp.bfloat16)
    return high, low


def dot3(left, right, dims):
    def one(a, b):
        return lax.dot_general(a, b, (dims, ((), ())), preferred_element_type=jnp.float32)

    return one(left[0], right[0]) + (one(left[0], right[1]) + one(left[1], right[0]))


NN = ((1,), (0,))
NT = ((1,), (1,))


def spline_weights(fractions):
    values = [fractions, 1.0 - fractions]
    for degree in (3, 4, 5):
        updated = []
        for position in range(degree):
            term = None
            if position < degree - 1:
                term = (fractions + position) * values[position]
            if position >= 1:
                lower = (degree - fractions - position) * values[position - 1]
                term = lower if term is None else term + lower
            updated.append(term * (1.0 / (degree - 1)))
        values = updated
    return values


def window_weights(offset, weights):
    position = lax.broadcasted_iota(jnp.int32, (REACH, offset.shape[1]), 0)
    selected = 4 + offset - position
    total = jnp.zeros(selected.shape, jnp.float32)
    for degree in range(5):
        total = jnp.where(selected == degree, weights[degree], total)
    return total


def depth_weights(base, weights, size):
    level = lax.broadcasted_iota(jnp.int32, (size, base.shape[1]), 0)
    selected = (base + 2 - level) & (size - 1)
    total = jnp.zeros(selected.shape, jnp.float32)
    for degree in range(5):
        total = jnp.where(selected == degree, weights[degree], total)
    return total


def cell_tables(across, base_ref, cell, size):
    def row(values):
        return [value[cell : cell + 1, :] for value in values]

    window_x = window_weights(base_ref[0, 0, cell : cell + 1, :] & (CELL - 1), row(across[0]))
    window_y = window_weights(base_ref[1, 0, cell : cell + 1, :] & (CELL - 1), row(across[1]))
    depth = depth_weights(base_ref[2, 0, cell : cell + 1, :], row(across[2]), size)
    return window_x, window_y, halves(depth)


def spread_kernel(size, charge_ref, fraction_ref, base_ref, out_ref):
    row = pl.program_id(0)

    @pl.when(row == 0)
    def _():
        out_ref[...] = jnp.zeros_like(out_ref)

    across = [spline_weights(fraction_ref[dim, 0]) for dim in range(3)]
    charge = charge_ref[0]
    cells_y, slots = charge.shape
    for cell in range(cells_y):
        window_x, window_y, depth = cell_tables(across, base_ref, cell, size)
        loaded = charge[cell : cell + 1, :] * window_x
        lifted = (loaded[:, None, :] * window_y[None, :, :]).reshape(REACH * REACH, slots)
        patch = dot3(halves(lifted), depth, NT).reshape(REACH, REACH, size)
        span = (pl.ds(row * CELL, REACH), pl.ds(cell * CELL, REACH), slice(None))
        out_ref[span] = out_ref[span] + patch


def gather_kernel(size, fraction_ref, base_ref, grid_ref, out_ref):
    row = pl.program_id(0)
    across = [spline_weights(fraction_ref[dim, 0]) for dim in range(3)]
    cells_y, slots = fraction_ref.shape[2:]
    for cell in range(cells_y):
        window_x, window_y, depth = cell_tables(across, base_ref, cell, size)
        span = (pl.ds(row * CELL, REACH), pl.ds(cell * CELL, REACH), slice(None))
        window = grid_ref[span].reshape(REACH * REACH, size)
        value = dot3(halves(window), depth, NN).reshape(REACH, REACH, slots)
        value = jnp.sum(value * window_x[:, None, :], axis=0) * window_y
        out_ref[0, cell : cell + 1, :] = jnp.sum(value, axis=0, keepdims=True)


def depth_forward_kernel(grid_ref, table_ref, out_ref):
    extent_x, extent_y, size = grid_ref.shape
    pairs = extent_x // 2
    table = (table_ref[0], table_ref[1])
    for pair in range(pairs):
        block = grid_ref[2 * pair : 2 * pair + 2].reshape(2 * extent_y, size)
        out_ref[pl.ds(pair, size, stride=pairs), :] = dot3(table, halves(block), NT)


def depth_inverse_kernel(in_ref, table_ref, out_ref):
    extent_x, extent_y, size = out_ref.shape
    pairs = extent_x // 2
    table = (table_ref[0], table_ref[1])
    for pair in range(pairs):
        block = in_ref[pl.ds(pair, size, stride=pairs), :].T
        out_ref[2 * pair : 2 * pair + 2] = dot3(halves(block), table, NN).reshape(
            2, extent_y, size
        )


def exchange_kernel(
    count_x,
    count_y,
    send_ref,
    influence_ref,
    right_ref,
    back_ref,
    left_ref,
    left_back_ref,
    out_ref,
    taken,
    turned,
    other,
    taken_sent,
    taken_here,
    turned_sent,
    turned_here,
    plane_sent,
    plane_here,
):
    devices, planes, parts, pairs, lanes = send_ref.shape
    half = lanes // 2
    rows = count_x * pairs
    full_y = count_y * half
    full_x = 2 * rows
    my_x, my_y = lax.axis_index("px"), lax.axis_index("py")
    me = my_x * count_y + my_y
    start = jnp.where(me < devices // 2, 0, 1)

    def peer(step):
        index = lax.rem(me + step, devices)
        return index, (index // count_y, lax.rem(index, count_y))

    barrier = pltpu.get_barrier_semaphore()

    @pl.loop(1, devices)
    def _(step):
        pl.semaphore_signal(barrier, inc=1, device_id=peer(step)[1], device_id_type=MESH)

    pl.semaphore_wait(barrier, devices - 1)

    lone = pltpu.make_async_remote_copy(
        src_ref=influence_ref.at[0],
        dst_ref=other,
        send_sem=plane_sent,
        recv_sem=plane_here,
        device_id=(0, 0),
        device_id_type=MESH,
    )

    @pl.when(me == devices // 2)
    def _():
        lone.start()

    @pl.loop(0, planes)
    def _(plane):
        @pl.loop(1, devices)
        def _(step):
            index, place = peer(step)
            pltpu.make_async_remote_copy(
                src_ref=send_ref.at[index, plane],
                dst_ref=taken.at[plane, me],
                send_sem=taken_sent.at[plane],
                recv_sem=taken_here.at[plane],
                device_id=place,
                device_id_type=MESH,
            ).start()

        taken[plane, me] = send_ref[me, plane]

    @pl.when(me == devices // 2)
    def _():
        lone.wait_send()

    @pl.when(me == 0)
    def _():
        lone.wait_recv()

    @pl.when(me != 0)
    def _():
        other[...] = influence_ref[start]

    def others(buffer, plane, sent, here):
        chunk = buffer.at[plane, pl.ds(0, devices - 1)]
        return pltpu.make_async_remote_copy(
            src_ref=chunk,
            dst_ref=chunk,
            send_sem=sent.at[plane],
            recv_sem=here.at[plane],
            device_id=peer(1)[1],
            device_id_type=MESH,
        )

    right = (right_ref[0], right_ref[1])
    back = (back_ref[0], back_ref[1])
    left = (left_ref[0], left_ref[1])
    left_back = (left_back_ref[0], left_back_ref[1])

    def load(plane, part):
        columns = [
            jnp.concatenate(
                [taken[plane, x * count_y + y, part] for x in range(count_x)], axis=0
            )
            for y in range(count_y)
        ]
        top = jnp.concatenate([block[:, :half] for block in columns], axis=1)
        bottom = jnp.concatenate([block[:, half:] for block in columns], axis=1)
        return jnp.concatenate([top, bottom], axis=0)

    def along_x(table, real, imag):
        both = dot3(table, halves(jnp.concatenate([real, imag], axis=1)), NN)
        upper, lower = both[:full_x], both[full_x:]
        return (
            upper[:, :full_y] - lower[:, full_y:],
            upper[:, full_y:] + lower[:, :full_y],
        )

    @pl.loop(0, planes)
    def _(plane):
        others(taken, plane, taken_sent, taken_here).wait_recv()
        first = dot3(halves(load(plane, 0)), right, NN)
        second = dot3(halves(load(plane, 1)), right, NN)
        ar, ai = along_x(left, first[:, :full_y], first[:, full_y:])
        br, bi = along_x(left, second[:, :full_y], second[:, full_y:])
        own = influence_ref[start + plane]
        mate = jnp.where(plane == 0, other[...], own)
        real, imag = along_x(left_back, own * ar - mate * bi, own * ai + mate * br)
        both = dot3(halves(jnp.concatenate([real, imag], axis=0)), back, NN)
        upper, lower = both[:full_x], both[full_x:]
        results = (
            upper[:, :full_y] - lower[:, full_y:],
            upper[:, full_y:] + lower[:, :full_y],
        )
        for part in range(2):
            result = results[part]
            for y in range(count_y):
                columns = slice(y * half, (y + 1) * half)
                block = jnp.concatenate(
                    [result[:rows, columns], result[rows:, columns]], axis=1
                ).reshape(count_x, pairs, lanes)
                for x in range(count_x):
                    turned[plane, x * count_y + y, part] = block[x]

        @pl.loop(1, devices)
        def _(step):
            index, place = peer(step)
            pltpu.make_async_remote_copy(
                src_ref=turned.at[plane, index],
                dst_ref=out_ref.at[me, plane],
                send_sem=turned_sent.at[plane],
                recv_sem=turned_here.at[plane],
                device_id=place,
                device_id_type=MESH,
            ).start()

        out_ref[me, plane] = turned[plane, me]

    @pl.loop(0, planes)
    def _(plane):
        others(taken, plane, taken_sent, taken_here).wait_send()
        last = others(turned, plane, turned_sent, turned_here)
        last.wait_send()
        last.wait_recv()


def neighbour_copies(count_x, count_y, row_out, row_in, col_out, col_in, edge_out, edge_in, sent, here):
    my_x, my_y = lax.axis_index("px"), lax.axis_index("py")

    def place(dx, dy):
        return lax.rem(my_x + dx + count_x, count_x), lax.rem(my_y + dy + count_y, count_y)

    shifts = (-1, 1)
    plan = [(row_out.at[i], row_in.at[i], place(shifts[i], 0)) for i in range(2)]
    plan += [(col_out.at[i], col_in.at[i], place(0, shifts[i])) for i in range(2)]
    plan += [
        (edge_out.at[2 * i + j], edge_in.at[2 * i + j], place(shifts[i], shifts[j]))
        for i in range(2)
        for j in range(2)
    ]
    barrier = pltpu.get_barrier_semaphore()
    for _, _, device in plan:
        pl.semaphore_signal(barrier, inc=1, device_id=device, device_id_type=MESH)
    pl.semaphore_wait(barrier, len(plan))
    copies = [
        pltpu.make_async_remote_copy(
            src_ref=source,
            dst_ref=target,
            send_sem=sent.at[k],
            recv_sem=here.at[k],
            device_id=device,
            device_id_type=MESH,
        )
        for k, (source, target, device) in enumerate(plan)
    ]
    return copies


def fold_kernel(count_x, count_y, in_ref, out_ref, *scratch):
    row_out, row_in, col_out, col_in, edge_out, edge_in, sent, here = scratch
    nx, ny, size = out_ref.shape
    for i in range(2):
        x = (0, nx + 2)[i]
        y = (0, ny + 2)[i]
        row_out[i] = in_ref[x : x + 2, 2 : ny + 2, :]
        for j in range(2):
            col_out[i, j] = in_ref[2 : nx + 2, y + j, :]
            edge = (0, ny + 2)[j]
            for k in range(2):
                edge_out[2 * i + j, 2 * k : 2 * k + 2] = in_ref[x + k, edge : edge + 2, :]
    copies = neighbour_copies(count_x, count_y, *scratch)
    for copy in copies:
        copy.start()
    out_ref[...] = in_ref[2 : nx + 2, 2 : ny + 2, :]
    for copy in copies:
        copy.wait()
    for i in range(2):
        x = (nx - 2, 0)[i]
        y = (ny - 2, 0)[i]
        out_ref[x : x + 2] = out_ref[x : x + 2] + row_in[i]
        for j in range(2):
            out_ref[:, y + j, :] = out_ref[:, y + j, :] + col_in[i, j]
            edge = (ny - 2, 0)[j]
            for k in range(2):
                out_ref[x + k, edge : edge + 2, :] = (
                    out_ref[x + k, edge : edge + 2, :] + edge_in[2 * i + j, 2 * k : 2 * k + 2]
                )


def halo_kernel(count_x, count_y, in_ref, out_ref, *scratch):
    row_out, row_in, col_out, col_in, edge_out, edge_in, sent, here = scratch
    nx, ny, size = in_ref.shape
    for i in range(2):
        x = (0, nx - 2)[i]
        y = (0, ny - 2)[i]
        row_out[i] = in_ref[x : x + 2]
        for j in range(2):
            col_out[i, j] = in_ref[:, y + j, :]
            edge = (0, ny - 2)[j]
            for k in range(2):
                edge_out[2 * i + j, 2 * k : 2 * k + 2] = in_ref[x + k, edge : edge + 2, :]
    copies = neighbour_copies(count_x, count_y, *scratch)
    for copy in copies:
        copy.start()
    out_ref[2 : nx + 2, 2 : ny + 2, :] = in_ref[...]
    for copy in copies:
        copy.wait()
    for i in range(2):
        x = (nx + 2, 0)[i]
        y = (ny + 2, 0)[i]
        out_ref[x : x + 2, 2 : ny + 2, :] = row_in[i]
        for j in range(2):
            out_ref[2 : nx + 2, y + j, :] = col_in[i, j]
            edge = (ny + 2, 0)[j]
            for k in range(2):
                out_ref[x + k, edge : edge + 2, :] = edge_in[2 * i + j, 2 * k : 2 * k + 2]


def halo_scratch(nx, ny, size):
    shapes = [(2, 2, ny, size)] * 2 + [(2, 2, nx, size)] * 2 + [(4, 4, size)] * 2
    return [pltpu.VMEM(shape, jnp.float32) for shape in shapes] + [
        pltpu.SemaphoreType.DMA((8,)),
        pltpu.SemaphoreType.DMA((8,)),
    ]


def wave_tables(size, devices, scale):
    each = size // devices
    rows, weights = [], []
    points = np.arange(size)
    for device in range(devices):
        for plane in range(each // 2):
            wave = device * each + plane + (0 if device < devices // 2 else 1)
            angle = (wave * points % size) * (2.0 * math.pi / size)
            if wave == 0:
                rows += [np.ones(size), 1.0 - 2.0 * (points % 2)]
                weights += [1.0, 1.0]
            else:
                rows += [np.cos(angle), -np.sin(angle)]
                weights += [2.0, 2.0]
    forward = np.stack(rows)
    return forward, forward * (np.array(weights)[:, None] * scale)


def angles(first, second, size):
    return (first[:, None] * second[None, :] % size) * (2.0 * math.pi / size)


def per_device(cotangent, fraction, grid_base, cell_count, influence):
    cells_x, cells_y, slots = cotangent.shape
    full_x, full_y = influence.shape[1:]
    px_size = lax.axis_size("px")
    py_size = lax.axis_size("py")
    devices = px_size * py_size
    each = influence.shape[0]
    size = each * devices
    planes = each // 2
    local_x = cells_x * CELL
    local_y = cells_y * CELL
    pairs = local_x // 2
    lanes = 2 * local_y
    params = pltpu.CompilerParams(vmem_limit_bytes=VMEM_LIMIT)
    occupied = jnp.arange(slots, dtype=jnp.int32)[None, None, :] < cell_count[:, :, None]
    charge = jnp.where(occupied, cotangent, 0.0)

    def linked(number):
        return pltpu.CompilerParams(
            vmem_limit_bytes=VMEM_LIMIT, collective_id=number, has_side_effects=True
        )

    whole = lambda *dims: pl.BlockSpec(dims, lambda *_: (0,) * len(dims))
    atoms = pl.BlockSpec((3, 1, cells_y, slots), lambda i: (0, i, 0, 0))
    cells = pl.BlockSpec((1, cells_y, slots), lambda i: (i, 0, 0))

    extended = pl.pallas_call(
        functools.partial(spread_kernel, size),
        grid=(cells_x,),
        in_specs=[cells, atoms, atoms],
        out_specs=whole(local_x + 4, local_y + 4, size),
        out_shape=jax.ShapeDtypeStruct((local_x + 4, local_y + 4, size), jnp.float32),
        compiler_params=params,
        name="spread",
    )(charge, fraction, grid_base)
    spread = pl.pallas_call(
        functools.partial(fold_kernel, px_size, py_size),
        out_shape=jax.ShapeDtypeStruct((local_x, local_y, size), jnp.float32),
        scratch_shapes=halo_scratch(local_x, local_y, size),
        compiler_params=linked(0),
        name="fold",
    )(extended)

    forward_z, inverse_z = wave_tables(size, devices, 1.0 / (size * full_x * full_y))
    columns = pl.pallas_call(
        depth_forward_kernel,
        out_shape=jax.ShapeDtypeStruct((size * pairs, lanes), jnp.float32),
        compiler_params=params,
        name="depth_forward",
    )(spread, halves_np(forward_z))
    order = np.arange(full_x).reshape(full_x // 2, 2).T.reshape(-1)
    y_angles = angles(np.arange(full_y), np.arange(full_y), full_y)
    x_angles = angles(np.arange(full_x), order, full_x)
    right = np.concatenate([np.cos(y_angles), -np.sin(y_angles)], axis=1)
    back = np.concatenate([np.cos(y_angles), np.sin(y_angles)], axis=1)
    left = np.concatenate([np.cos(x_angles), -np.sin(x_angles)], axis=0)
    left_back = np.concatenate([np.cos(x_angles.T), np.sin(x_angles.T)], axis=0)
    chunks = (devices, planes, 2, pairs, lanes)
    landing = pltpu.VMEM((planes, devices, 2, pairs, lanes), jnp.float32)
    in_vmem = pl.BlockSpec(memory_space=pltpu.VMEM)
    returned = pl.pallas_call(
        functools.partial(exchange_kernel, px_size, py_size),
        in_specs=[in_vmem] * 6,
        out_specs=in_vmem,
        out_shape=jax.ShapeDtypeStruct(chunks, jnp.float32),
        scratch_shapes=[landing, landing, pltpu.VMEM((full_x, full_y), jnp.float32)]
        + [pltpu.SemaphoreType.DMA((planes,))] * 4
        + [pltpu.SemaphoreType.DMA] * 2,
        compiler_params=linked(1),
        name="exchange",
    )(
        columns.reshape(chunks),
        influence,
        halves_np(right),
        halves_np(back),
        halves_np(left),
        halves_np(left_back),
    ).reshape(size * pairs, lanes)
    potential = pl.pallas_call(
        depth_inverse_kernel,
        out_shape=jax.ShapeDtypeStruct((local_x, local_y, size), jnp.float32),
        compiler_params=params,
        name="depth_inverse",
    )(returned, halves_np(inverse_z))
    halo_potential = pl.pallas_call(
        functools.partial(halo_kernel, px_size, py_size),
        out_shape=jax.ShapeDtypeStruct(extended.shape, jnp.float32),
        scratch_shapes=halo_scratch(local_x, local_y, size),
        compiler_params=linked(2),
        name="halo",
    )(potential)
    gradient = pl.pallas_call(
        functools.partial(gather_kernel, size),
        grid=(cells_x,),
        in_specs=[atoms, atoms, whole(local_x + 4, local_y + 4, size)],
        out_specs=cells,
        out_shape=jax.ShapeDtypeStruct(cotangent.shape, jnp.float32),
        compiler_params=params,
        name="gather",
    )(fraction, grid_base, halo_potential)
    return jnp.where(occupied, gradient, 0.0)


def solution(mesh):
    placed = (
        P("px", "py", None),
        P(None, "px", "py", None),
        P(None, "px", "py", None),
        P("px", "py"),
        P(("px", "py"), None, None),
    )
    return jax.shard_map(
        per_device, mesh=mesh, in_specs=placed, out_specs=P("px", "py", None), check_vma=False
    )
```

```python
import functools
import math

import jax
import jax.numpy as jnp
import ml_dtypes
import numpy as np
from jax import lax
from jax.experimental import pallas as pl
from jax.experimental.pallas import tpu as pltpu
from jax.sharding import PartitionSpec as P

CELL = 4
REACH = 8
VMEM_LIMIT = 48 * 1024 * 1024
MESH = pl.DeviceIdType.MESH


def halves_np(table):
    high = np.asarray(table, np.float32).astype(ml_dtypes.bfloat16)
    low = (np.asarray(table, np.float64) - high.astype(np.float64)).astype(ml_dtypes.bfloat16)
    return jnp.asarray(np.stack([high, low]))


def halves(value):
    high = value.astype(jnp.bfloat16)
    low = (value - high.astype(jnp.float32)).astype(jnp.bfloat16)
    return high, low


def dot3(left, right, dims):
    def one(a, b):
        return lax.dot_general(a, b, (dims, ((), ())), preferred_element_type=jnp.float32)

    return one(left[0], right[0]) + (one(left[0], right[1]) + one(left[1], right[0]))


NN = ((1,), (0,))
NT = ((1,), (1,))


def spline_weights(fractions):
    values = [fractions, 1.0 - fractions]
    for degree in (3, 4, 5):
        updated = []
        for position in range(degree):
            term = None
            if position < degree - 1:
                term = (fractions + position) * values[position]
            if position >= 1:
                lower = (degree - fractions - position) * values[position - 1]
                term = lower if term is None else term + lower
            updated.append(term * (1.0 / (degree - 1)))
        values = updated
    return values


def window_weights(offset, weights):
    position = lax.broadcasted_iota(jnp.int32, (REACH, offset.shape[1]), 0)
    selected = 4 + offset - position
    total = jnp.zeros(selected.shape, jnp.float32)
    for degree in range(5):
        total = jnp.where(selected == degree, weights[degree], total)
    return total


def depth_weights(base, weights, size):
    slots = base.shape[1]
    tile, shape = (16, slots), (size // 16, 16, slots)
    inner = lax.broadcasted_iota(jnp.int32, tile, 0)
    anchor = (jnp.broadcast_to(base + 2, tile) - inner).astype(jnp.int16)[None]
    level = (16 * lax.broadcasted_iota(jnp.int32, shape, 0)).astype(jnp.int16)
    selected = (anchor - level) & jnp.int16(size - 1)
    high = jnp.zeros(shape, jnp.bfloat16)
    low = jnp.zeros(shape, jnp.bfloat16)
    for degree in range(5):
        here = selected == jnp.int16(degree)
        upper, lower = halves(jnp.broadcast_to(weights[degree], tile))
        high = jnp.where(here, upper[None], high)
        low = jnp.where(here, lower[None], low)
    return high.reshape(size, slots), low.reshape(size, slots)


def cell_tables(across, base_ref, index, cell, size):
    def row(values):
        return [value[cell : cell + 1, :] for value in values]

    def base(dim):
        return base_ref[dim, index, cell : cell + 1, :]

    window_x = window_weights(base(0) & (CELL - 1), row(across[0]))
    window_y = window_weights(base(1) & (CELL - 1), row(across[1]))
    return window_x, window_y, depth_weights(base(2), row(across[2]), size)


def border_rows(body, cells_x, cells_y):
    @pl.loop(0, 2)
    def _(side):
        body(side * (cells_x - 1), range(cells_y))

    @pl.loop(1, cells_x - 1)
    def _(row):
        body(row, (0, cells_y - 1))


def inner_rows(body, cells_x, cells_y):
    @pl.loop(1, cells_x - 1)
    def _(row):
        body(row, range(1, cells_y - 1))


def depth_forward_kernel(grid_ref, table_ref, out_ref):
    extent_x, extent_y, size = grid_ref.shape
    pairs = extent_x // 2
    table = (table_ref[0], table_ref[1])
    for pair in range(pairs):
        block = grid_ref[2 * pair : 2 * pair + 2].reshape(2 * extent_y, size)
        out_ref[pl.ds(pair, size, stride=pairs), :] = dot3(table, halves(block), NT)


def depth_inverse_kernel(in_ref, table_ref, out_ref):
    extent_x, extent_y, size = out_ref.shape
    pairs = extent_x // 2
    table = (table_ref[0], table_ref[1])
    for pair in range(pairs):
        block = in_ref[pl.ds(pair, size, stride=pairs), :].T
        out_ref[2 * pair : 2 * pair + 2] = dot3(halves(block), table, NN).reshape(
            2, extent_y, size
        )


def exchange_kernel(
    count_x,
    count_y,
    send_ref,
    influence_ref,
    right_ref,
    back_ref,
    left_ref,
    left_back_ref,
    out_ref,
    taken,
    turned,
    other,
    taken_sent,
    taken_here,
    turned_sent,
    turned_here,
    plane_sent,
    plane_here,
):
    devices, planes, parts, pairs, lanes = send_ref.shape
    half = lanes // 2
    rows = count_x * pairs
    full_y = count_y * half
    full_x = 2 * rows
    my_x, my_y = lax.axis_index("px"), lax.axis_index("py")
    me = my_x * count_y + my_y
    start = jnp.where(me < devices // 2, 0, 1)

    def peer(step):
        index = lax.rem(me + step, devices)
        return index, (index // count_y, lax.rem(index, count_y))

    barrier = pltpu.get_barrier_semaphore()

    @pl.loop(1, devices)
    def _(step):
        pl.semaphore_signal(barrier, inc=1, device_id=peer(step)[1], device_id_type=MESH)

    pl.semaphore_wait(barrier, devices - 1)

    lone = pltpu.make_async_remote_copy(
        src_ref=influence_ref.at[0],
        dst_ref=other,
        send_sem=plane_sent,
        recv_sem=plane_here,
        device_id=(0, 0),
        device_id_type=MESH,
    )

    @pl.when(me == devices // 2)
    def _():
        lone.start()

    @pl.loop(0, planes)
    def _(plane):
        @pl.loop(1, devices)
        def _(step):
            index, place = peer(step)
            pltpu.make_async_remote_copy(
                src_ref=send_ref.at[index, plane],
                dst_ref=taken.at[plane, me],
                send_sem=taken_sent.at[plane],
                recv_sem=taken_here.at[plane],
                device_id=place,
                device_id_type=MESH,
            ).start()

        taken[plane, me] = send_ref[me, plane]

    @pl.when(me == devices // 2)
    def _():
        lone.wait_send()

    @pl.when(me == 0)
    def _():
        lone.wait_recv()

    @pl.when(me != 0)
    def _():
        other[...] = influence_ref[start]

    def others(buffer, plane, sent, here):
        chunk = buffer.at[plane, pl.ds(0, devices - 1)]
        return pltpu.make_async_remote_copy(
            src_ref=chunk,
            dst_ref=chunk,
            send_sem=sent.at[plane],
            recv_sem=here.at[plane],
            device_id=peer(1)[1],
            device_id_type=MESH,
        )

    right = (right_ref[0], right_ref[1])
    back = (back_ref[0], back_ref[1])
    left = (left_ref[0], left_ref[1])
    left_back = (left_back_ref[0], left_back_ref[1])

    def load(plane, part):
        columns = [
            jnp.concatenate(
                [taken[plane, x * count_y + y, part] for x in range(count_x)], axis=0
            )
            for y in range(count_y)
        ]
        top = jnp.concatenate([block[:, :half] for block in columns], axis=1)
        bottom = jnp.concatenate([block[:, half:] for block in columns], axis=1)
        return jnp.concatenate([top, bottom], axis=0)

    def along_x(table, real, imag):
        both = dot3(table, halves(jnp.concatenate([real, imag], axis=1)), NN)
        upper, lower = both[:full_x], both[full_x:]
        return (
            upper[:, :full_y] - lower[:, full_y:],
            upper[:, full_y:] + lower[:, :full_y],
        )

    @pl.loop(0, planes)
    def _(plane):
        others(taken, plane, taken_sent, taken_here).wait_recv()
        first = dot3(halves(load(plane, 0)), right, NN)
        second = dot3(halves(load(plane, 1)), right, NN)
        ar, ai = along_x(left, first[:, :full_y], first[:, full_y:])
        br, bi = along_x(left, second[:, :full_y], second[:, full_y:])
        own = influence_ref[start + plane]
        mate = jnp.where(plane == 0, other[...], own)
        real, imag = along_x(left_back, own * ar - mate * bi, own * ai + mate * br)
        both = dot3(halves(jnp.concatenate([real, imag], axis=0)), back, NN)
        upper, lower = both[:full_x], both[full_x:]
        results = (
            upper[:, :full_y] - lower[:, full_y:],
            upper[:, full_y:] + lower[:, :full_y],
        )
        for part in range(2):
            result = results[part]
            for y in range(count_y):
                columns = slice(y * half, (y + 1) * half)
                block = jnp.concatenate(
                    [result[:rows, columns], result[rows:, columns]], axis=1
                ).reshape(count_x, pairs, lanes)
                for x in range(count_x):
                    turned[plane, x * count_y + y, part] = block[x]

        @pl.loop(1, devices)
        def _(step):
            index, place = peer(step)
            pltpu.make_async_remote_copy(
                src_ref=turned.at[plane, index],
                dst_ref=out_ref.at[me, plane],
                send_sem=turned_sent.at[plane],
                recv_sem=turned_here.at[plane],
                device_id=place,
                device_id_type=MESH,
            ).start()

        out_ref[me, plane] = turned[plane, me]

    @pl.loop(0, planes)
    def _(plane):
        others(taken, plane, taken_sent, taken_here).wait_send()
        last = others(turned, plane, turned_sent, turned_here)
        last.wait_send()
        last.wait_recv()


def neighbour_copies(count_x, count_y, row_out, row_in, col_out, col_in, edge_out, edge_in, sent, here):
    my_x, my_y = lax.axis_index("px"), lax.axis_index("py")

    def place(dx, dy):
        return lax.rem(my_x + dx + count_x, count_x), lax.rem(my_y + dy + count_y, count_y)

    shifts = (-1, 1)
    plan = [(row_out.at[i], row_in.at[i], place(shifts[i], 0)) for i in range(2)]
    plan += [(col_out.at[i], col_in.at[i], place(0, shifts[i])) for i in range(2)]
    plan += [
        (edge_out.at[2 * i + j], edge_in.at[2 * i + j], place(shifts[i], shifts[j]))
        for i in range(2)
        for j in range(2)
    ]
    barrier = pltpu.get_barrier_semaphore()
    for _, _, device in plan:
        pl.semaphore_signal(barrier, inc=1, device_id=device, device_id_type=MESH)
    pl.semaphore_wait(barrier, len(plan))
    copies = [
        pltpu.make_async_remote_copy(
            src_ref=source,
            dst_ref=target,
            send_sem=sent.at[k],
            recv_sem=here.at[k],
            device_id=device,
            device_id_type=MESH,
        )
        for k, (source, target, device) in enumerate(plan)
    ]
    return copies


def spread_kernel(
    count_x, count_y, charge_ref, fraction_ref, base_ref, out_ref, ext_ref, *scratch
):
    row_out, row_in, col_out, col_in, edge_out, edge_in, sent, here = scratch
    nx, ny, size = out_ref.shape
    cells_x, cells_y, slots = charge_ref.shape
    ext_ref[...] = jnp.zeros_like(ext_ref)

    def work(row, chosen):
        across = [spline_weights(fraction_ref[dim, row]) for dim in range(3)]
        charge = charge_ref[row]
        for cell in chosen:
            window_x, window_y, depth = cell_tables(across, base_ref, row, cell, size)
            loaded = charge[cell : cell + 1, :] * window_x
            lifted = (loaded[:, None, :] * window_y[None, :, :]).reshape(REACH * REACH, slots)
            patch = dot3(halves(lifted), depth, NT).reshape(REACH, REACH, size)
            span = (pl.ds(row * CELL, REACH), pl.ds(cell * CELL, REACH), slice(None))
            ext_ref[span] = ext_ref[span] + patch

    copies = neighbour_copies(count_x, count_y, *scratch)
    border_rows(work, cells_x, cells_y)
    for i in range(2):
        x = (0, nx + 2)[i]
        y = (0, ny + 2)[i]
        row_out[i] = ext_ref[x : x + 2, 2 : ny + 2, :]
        for j in range(2):
            col_out[i, j] = ext_ref[2 : nx + 2, y + j, :]
            edge = (0, ny + 2)[j]
            for k in range(2):
                edge_out[2 * i + j, 2 * k : 2 * k + 2] = ext_ref[x + k, edge : edge + 2, :]
    for copy in copies:
        copy.start()
    inner_rows(work, cells_x, cells_y)
    out_ref[...] = ext_ref[2 : nx + 2, 2 : ny + 2, :]
    for copy in copies:
        copy.wait()
    for i in range(2):
        x = (nx - 2, 0)[i]
        y = (ny - 2, 0)[i]
        out_ref[x : x + 2] = out_ref[x : x + 2] + row_in[i]
        for j in range(2):
            out_ref[:, y + j, :] = out_ref[:, y + j, :] + col_in[i, j]
            edge = (ny - 2, 0)[j]
            for k in range(2):
                out_ref[x + k, edge : edge + 2, :] = (
                    out_ref[x + k, edge : edge + 2, :] + edge_in[2 * i + j, 2 * k : 2 * k + 2]
                )


def gather_kernel(
    count_x, count_y, fraction_ref, base_ref, in_ref, out_ref, ext_ref, *scratch
):
    row_out, row_in, col_out, col_in, edge_out, edge_in, sent, here = scratch
    nx, ny, size = in_ref.shape
    cells_x, cells_y, slots = out_ref.shape

    def work(row, chosen):
        across = [spline_weights(fraction_ref[dim, row]) for dim in range(3)]
        for cell in chosen:
            window_x, window_y, depth = cell_tables(across, base_ref, row, cell, size)
            span = (pl.ds(row * CELL, REACH), pl.ds(cell * CELL, REACH), slice(None))
            window = ext_ref[span].reshape(REACH * REACH, size)
            value = dot3(halves(window), depth, NN).reshape(REACH, REACH, slots)
            value = jnp.sum(value * window_x[:, None, :], axis=0) * window_y
            out_ref[row, cell : cell + 1, :] = jnp.sum(value, axis=0, keepdims=True)

    for i in range(2):
        x = (0, nx - 2)[i]
        y = (0, ny - 2)[i]
        row_out[i] = in_ref[x : x + 2]
        for j in range(2):
            col_out[i, j] = in_ref[:, y + j, :]
            edge = (0, ny - 2)[j]
            for k in range(2):
                edge_out[2 * i + j, 2 * k : 2 * k + 2] = in_ref[x + k, edge : edge + 2, :]
    copies = neighbour_copies(count_x, count_y, *scratch)
    for copy in copies:
        copy.start()
    ext_ref[2 : nx + 2, 2 : ny + 2, :] = in_ref[...]
    inner_rows(work, cells_x, cells_y)
    for copy in copies:
        copy.wait()
    for i in range(2):
        x = (nx + 2, 0)[i]
        y = (ny + 2, 0)[i]
        ext_ref[x : x + 2, 2 : ny + 2, :] = row_in[i]
        for j in range(2):
            ext_ref[2 : nx + 2, y + j, :] = col_in[i, j]
            edge = (ny + 2, 0)[j]
            for k in range(2):
                ext_ref[x + k, edge : edge + 2, :] = edge_in[2 * i + j, 2 * k : 2 * k + 2]
    border_rows(work, cells_x, cells_y)


def halo_scratch(nx, ny, size):
    shapes = [(2, 2, ny, size)] * 2 + [(2, 2, nx, size)] * 2 + [(4, 4, size)] * 2
    shapes = [(nx + 4, ny + 4, size)] + shapes
    return [pltpu.VMEM(shape, jnp.float32) for shape in shapes] + [
        pltpu.SemaphoreType.DMA((8,)),
        pltpu.SemaphoreType.DMA((8,)),
    ]


def wave_tables(size, devices, scale):
    each = size // devices
    rows, weights = [], []
    points = np.arange(size)
    for device in range(devices):
        for plane in range(each // 2):
            wave = device * each + plane + (0 if device < devices // 2 else 1)
            angle = (wave * points % size) * (2.0 * math.pi / size)
            if wave == 0:
                rows += [np.ones(size), 1.0 - 2.0 * (points % 2)]
                weights += [1.0, 1.0]
            else:
                rows += [np.cos(angle), -np.sin(angle)]
                weights += [2.0, 2.0]
    forward = np.stack(rows)
    return forward, forward * (np.array(weights)[:, None] * scale)


def angles(first, second, size):
    return (first[:, None] * second[None, :] % size) * (2.0 * math.pi / size)


def per_device(cotangent, fraction, grid_base, cell_count, influence):
    cells_x, cells_y, slots = cotangent.shape
    full_x, full_y = influence.shape[1:]
    px_size = lax.axis_size("px")
    py_size = lax.axis_size("py")
    devices = px_size * py_size
    each = influence.shape[0]
    size = each * devices
    planes = each // 2
    local_x = cells_x * CELL
    local_y = cells_y * CELL
    pairs = local_x // 2
    lanes = 2 * local_y
    params = pltpu.CompilerParams(vmem_limit_bytes=VMEM_LIMIT)
    occupied = jnp.arange(slots, dtype=jnp.int32)[None, None, :] < cell_count[:, :, None]
    charge = jnp.where(occupied, cotangent, 0.0)

    def linked(number):
        return pltpu.CompilerParams(
            vmem_limit_bytes=VMEM_LIMIT, collective_id=number, has_side_effects=True
        )

    spread = pl.pallas_call(
        functools.partial(spread_kernel, px_size, py_size),
        out_shape=jax.ShapeDtypeStruct((local_x, local_y, size), jnp.float32),
        scratch_shapes=halo_scratch(local_x, local_y, size),
        compiler_params=linked(0),
        name="spread",
    )(charge, fraction, grid_base)

    forward_z, inverse_z = wave_tables(size, devices, 1.0 / (size * full_x * full_y))
    columns = pl.pallas_call(
        depth_forward_kernel,
        out_shape=jax.ShapeDtypeStruct((size * pairs, lanes), jnp.float32),
        compiler_params=params,
        name="depth_forward",
    )(spread, halves_np(forward_z))
    order = np.arange(full_x).reshape(full_x // 2, 2).T.reshape(-1)
    y_angles = angles(np.arange(full_y), np.arange(full_y), full_y)
    x_angles = angles(np.arange(full_x), order, full_x)
    right = np.concatenate([np.cos(y_angles), -np.sin(y_angles)], axis=1)
    back = np.concatenate([np.cos(y_angles), np.sin(y_angles)], axis=1)
    left = np.concatenate([np.cos(x_angles), -np.sin(x_angles)], axis=0)
    left_back = np.concatenate([np.cos(x_angles.T), np.sin(x_angles.T)], axis=0)
    chunks = (devices, planes, 2, pairs, lanes)
    landing = pltpu.VMEM((planes, devices, 2, pairs, lanes), jnp.float32)
    in_vmem = pl.BlockSpec(memory_space=pltpu.VMEM)
    returned = pl.pallas_call(
        functools.partial(exchange_kernel, px_size, py_size),
        in_specs=[in_vmem] * 6,
        out_specs=in_vmem,
        out_shape=jax.ShapeDtypeStruct(chunks, jnp.float32),
        scratch_shapes=[landing, landing, pltpu.VMEM((full_x, full_y), jnp.float32)]
        + [pltpu.SemaphoreType.DMA((planes,))] * 4
        + [pltpu.SemaphoreType.DMA] * 2,
        compiler_params=linked(1),
        name="exchange",
    )(
        columns.reshape(chunks),
        influence,
        halves_np(right),
        halves_np(back),
        halves_np(left),
        halves_np(left_back),
    ).reshape(size * pairs, lanes)
    potential = pl.pallas_call(
        depth_inverse_kernel,
        out_shape=jax.ShapeDtypeStruct((local_x, local_y, size), jnp.float32),
        compiler_params=params,
        name="depth_inverse",
    )(returned, halves_np(inverse_z))
    gradient = pl.pallas_call(
        functools.partial(gather_kernel, px_size, py_size),
        out_shape=jax.ShapeDtypeStruct(cotangent.shape, jnp.float32),
        scratch_shapes=halo_scratch(local_x, local_y, size),
        compiler_params=linked(2),
        name="gather",
    )(fraction, grid_base, potential)
    return jnp.where(occupied, gradient, 0.0)


def solution(mesh):
    placed = (
        P("px", "py", None),
        P(None, "px", "py", None),
        P(None, "px", "py", None),
        P("px", "py"),
        P(("px", "py"), None, None),
    )
    return jax.shard_map(
        per_device, mesh=mesh, in_specs=placed, out_specs=P("px", "py", None), check_vma=False
    )
```

```python
import functools
import math

import jax
import jax.numpy as jnp
import ml_dtypes
import numpy as np
from jax import lax
from jax.experimental import pallas as pl
from jax.experimental.pallas import tpu as pltpu
from jax.sharding import PartitionSpec as P

CELL = 4
REACH = 8
VMEM_LIMIT = 48 * 1024 * 1024
MESH = pl.DeviceIdType.MESH


def halves_np(table):
    high = np.asarray(table, np.float32).astype(ml_dtypes.bfloat16)
    low = (np.asarray(table, np.float64) - high.astype(np.float64)).astype(ml_dtypes.bfloat16)
    return jnp.asarray(np.stack([high, low]))


def halves(value):
    high = value.astype(jnp.bfloat16)
    low = (value - high.astype(jnp.float32)).astype(jnp.bfloat16)
    return high, low


def dot3(left, right, dims):
    def one(a, b):
        return lax.dot_general(a, b, (dims, ((), ())), preferred_element_type=jnp.float32)

    rows = left[0].shape[0]
    both = one(jnp.concatenate(left, axis=0), right[0])
    return both[:rows] + (one(left[0], right[1]) + both[rows:])


NN = ((1,), (0,))
NT = ((1,), (1,))


def spline_weights(fractions):
    values = [fractions, 1.0 - fractions]
    for degree in (3, 4, 5):
        updated = []
        for position in range(degree):
            term = None
            if position < degree - 1:
                term = (fractions + position) * values[position]
            if position >= 1:
                lower = (degree - fractions - position) * values[position - 1]
                term = lower if term is None else term + lower
            updated.append(term * (1.0 / (degree - 1)))
        values = updated
    return values


def window_weights(offset, weights):
    position = lax.broadcasted_iota(jnp.int32, (REACH, offset.shape[1]), 0)
    selected = 4 + offset - position
    total = jnp.zeros(selected.shape, jnp.float32)
    for degree in range(5):
        total = jnp.where(selected == degree, weights[degree], total)
    return total


def depth_weights(base, weights, size):
    slots = base.shape[1]
    tile, shape = (16, slots), (size // 16, 16, slots)
    inner = lax.broadcasted_iota(jnp.int32, tile, 0)
    anchor = (jnp.broadcast_to(base + 2, tile) - inner).astype(jnp.int16)[None]
    level = (16 * lax.broadcasted_iota(jnp.int32, shape, 0)).astype(jnp.int16)
    selected = (anchor - level) & jnp.int16(size - 1)
    high = jnp.zeros(shape, jnp.bfloat16)
    low = jnp.zeros(shape, jnp.bfloat16)
    for degree in range(5):
        here = selected == jnp.int16(degree)
        upper, lower = halves(jnp.broadcast_to(weights[degree], tile))
        high = jnp.where(here, upper[None], high)
        low = jnp.where(here, lower[None], low)
    return high.reshape(size, slots), low.reshape(size, slots)


def cell_tables(across, base_ref, index, cell, size):
    def row(values):
        return [value[cell : cell + 1, :] for value in values]

    def base(dim):
        return base_ref[dim, index, cell : cell + 1, :]

    window_x = window_weights(base(0) & (CELL - 1), row(across[0]))
    window_y = window_weights(base(1) & (CELL - 1), row(across[1]))
    return window_x, window_y, depth_weights(base(2), row(across[2]), size)


def border_rows(body, cells_x, cells_y):
    @pl.loop(0, 2)
    def _(side):
        body(side * (cells_x - 1), range(cells_y))

    @pl.loop(1, cells_x - 1)
    def _(row):
        body(row, (0, cells_y - 1))


def inner_rows(body, cells_x, cells_y):
    @pl.loop(1, cells_x - 1)
    def _(row):
        body(row, range(1, cells_y - 1))


def depth_forward_kernel(grid_ref, table_ref, out_ref):
    extent_x, extent_y, size = grid_ref.shape
    pairs = extent_x // 2
    table = (table_ref[0], table_ref[1])
    for pair in range(pairs):
        block = grid_ref[2 * pair : 2 * pair + 2].reshape(2 * extent_y, size)
        out_ref[pl.ds(pair, size, stride=pairs), :] = dot3(table, halves(block), NT)


def depth_inverse_kernel(in_ref, table_ref, out_ref):
    extent_x, extent_y, size = out_ref.shape
    pairs = extent_x // 2
    table = (table_ref[0], table_ref[1])
    for pair in range(pairs):
        block = in_ref[pl.ds(pair, size, stride=pairs), :].T
        out_ref[2 * pair : 2 * pair + 2] = dot3(halves(block), table, NN).reshape(
            2, extent_y, size
        )


def exchange_kernel(
    count_x,
    count_y,
    send_ref,
    influence_ref,
    right_ref,
    back_ref,
    left_ref,
    left_back_ref,
    out_ref,
    taken,
    turned,
    other,
    taken_sent,
    taken_here,
    turned_sent,
    turned_here,
    plane_sent,
    plane_here,
):
    devices, planes, parts, pairs, lanes = send_ref.shape
    half = lanes // 2
    rows = count_x * pairs
    full_y = count_y * half
    full_x = 2 * rows
    my_x, my_y = lax.axis_index("px"), lax.axis_index("py")
    me = my_x * count_y + my_y
    start = jnp.where(me < devices // 2, 0, 1)

    def peer(step):
        index = lax.rem(me + step, devices)
        return index, (index // count_y, lax.rem(index, count_y))

    barrier = pltpu.get_barrier_semaphore()

    @pl.loop(1, devices)
    def _(step):
        pl.semaphore_signal(barrier, inc=1, device_id=peer(step)[1], device_id_type=MESH)

    pl.semaphore_wait(barrier, devices - 1)

    lone = pltpu.make_async_remote_copy(
        src_ref=influence_ref.at[0],
        dst_ref=other,
        send_sem=plane_sent,
        recv_sem=plane_here,
        device_id=(0, 0),
        device_id_type=MESH,
    )

    @pl.when(me == devices // 2)
    def _():
        lone.start()

    @pl.loop(0, planes)
    def _(plane):
        @pl.loop(1, devices)
        def _(step):
            index, place = peer(step)
            pltpu.make_async_remote_copy(
                src_ref=send_ref.at[index, plane],
                dst_ref=taken.at[plane, me],
                send_sem=taken_sent.at[plane],
                recv_sem=taken_here.at[plane],
                device_id=place,
                device_id_type=MESH,
            ).start()

        taken[plane, me] = send_ref[me, plane]

    @pl.when(me == devices // 2)
    def _():
        lone.wait_send()

    @pl.when(me == 0)
    def _():
        lone.wait_recv()

    @pl.when(me != 0)
    def _():
        other[...] = influence_ref[start]

    def others(buffer, plane, sent, here):
        chunk = buffer.at[plane, pl.ds(0, devices - 1)]
        return pltpu.make_async_remote_copy(
            src_ref=chunk,
            dst_ref=chunk,
            send_sem=sent.at[plane],
            recv_sem=here.at[plane],
            device_id=peer(1)[1],
            device_id_type=MESH,
        )

    right = (right_ref[0], right_ref[1])
    back = (back_ref[0], back_ref[1])
    left = (left_ref[0], left_ref[1])
    left_back = (left_back_ref[0], left_back_ref[1])

    def load(plane, part):
        columns = [
            jnp.concatenate(
                [taken[plane, x * count_y + y, part] for x in range(count_x)], axis=0
            )
            for y in range(count_y)
        ]
        top = jnp.concatenate([block[:, :half] for block in columns], axis=1)
        bottom = jnp.concatenate([block[:, half:] for block in columns], axis=1)
        return jnp.concatenate([top, bottom], axis=0)

    def along_x(table, real, imag):
        both = dot3(table, halves(jnp.concatenate([real, imag], axis=1)), NN)
        upper, lower = both[:full_x], both[full_x:]
        return (
            upper[:, :full_y] - lower[:, full_y:],
            upper[:, full_y:] + lower[:, :full_y],
        )

    @pl.loop(0, planes)
    def _(plane):
        others(taken, plane, taken_sent, taken_here).wait_recv()
        first = dot3(halves(load(plane, 0)), right, NN)
        second = dot3(halves(load(plane, 1)), right, NN)
        ar, ai = along_x(left, first[:, :full_y], first[:, full_y:])
        br, bi = along_x(left, second[:, :full_y], second[:, full_y:])
        own = influence_ref[start + plane]
        mate = jnp.where(plane == 0, other[...], own)
        real, imag = along_x(left_back, own * ar - mate * bi, own * ai + mate * br)
        both = dot3(halves(jnp.concatenate([real, imag], axis=0)), back, NN)
        upper, lower = both[:full_x], both[full_x:]
        results = (
            upper[:, :full_y] - lower[:, full_y:],
            upper[:, full_y:] + lower[:, :full_y],
        )
        for part in range(2):
            result = results[part]
            for y in range(count_y):
                columns = slice(y * half, (y + 1) * half)
                block = jnp.concatenate(
                    [result[:rows, columns], result[rows:, columns]], axis=1
                ).reshape(count_x, pairs, lanes)
                for x in range(count_x):
                    turned[plane, x * count_y + y, part] = block[x]

        @pl.loop(1, devices)
        def _(step):
            index, place = peer(step)
            pltpu.make_async_remote_copy(
                src_ref=turned.at[plane, index],
                dst_ref=out_ref.at[me, plane],
                send_sem=turned_sent.at[plane],
                recv_sem=turned_here.at[plane],
                device_id=place,
                device_id_type=MESH,
            ).start()

        out_ref[me, plane] = turned[plane, me]

    @pl.loop(0, planes)
    def _(plane):
        others(taken, plane, taken_sent, taken_here).wait_send()
        last = others(turned, plane, turned_sent, turned_here)
        last.wait_send()
        last.wait_recv()


def neighbour_copies(count_x, count_y, row_out, row_in, col_out, col_in, edge_out, edge_in, sent, here):
    my_x, my_y = lax.axis_index("px"), lax.axis_index("py")

    def place(dx, dy):
        return lax.rem(my_x + dx + count_x, count_x), lax.rem(my_y + dy + count_y, count_y)

    shifts = (-1, 1)
    plan = [(row_out.at[i], row_in.at[i], place(shifts[i], 0)) for i in range(2)]
    plan += [(col_out.at[i], col_in.at[i], place(0, shifts[i])) for i in range(2)]
    plan += [
        (edge_out.at[2 * i + j], edge_in.at[2 * i + j], place(shifts[i], shifts[j]))
        for i in range(2)
        for j in range(2)
    ]
    barrier = pltpu.get_barrier_semaphore()
    for _, _, device in plan:
        pl.semaphore_signal(barrier, inc=1, device_id=device, device_id_type=MESH)
    pl.semaphore_wait(barrier, len(plan))
    copies = [
        pltpu.make_async_remote_copy(
            src_ref=source,
            dst_ref=target,
            send_sem=sent.at[k],
            recv_sem=here.at[k],
            device_id=device,
            device_id_type=MESH,
        )
        for k, (source, target, device) in enumerate(plan)
    ]
    return copies


def spread_kernel(
    count_x, count_y, charge_ref, fraction_ref, base_ref, out_ref, ext_ref, *scratch
):
    row_out, row_in, col_out, col_in, edge_out, edge_in, sent, here = scratch
    nx, ny, size = out_ref.shape
    cells_x, cells_y, slots = charge_ref.shape
    ext_ref[...] = jnp.zeros_like(ext_ref)

    def work(row, chosen):
        across = [spline_weights(fraction_ref[dim, row]) for dim in range(3)]
        charge = charge_ref[row]
        for cell in chosen:
            window_x, window_y, depth = cell_tables(across, base_ref, row, cell, size)
            loaded = charge[cell : cell + 1, :] * window_x
            lifted = (loaded[:, None, :] * window_y[None, :, :]).reshape(REACH * REACH, slots)
            patch = dot3(halves(lifted), depth, NT).reshape(REACH, REACH, size)
            span = (pl.ds(row * CELL, REACH), pl.ds(cell * CELL, REACH), slice(None))
            ext_ref[span] = ext_ref[span] + patch

    copies = neighbour_copies(count_x, count_y, *scratch)
    border_rows(work, cells_x, cells_y)
    for i in range(2):
        x = (0, nx + 2)[i]
        y = (0, ny + 2)[i]
        row_out[i] = ext_ref[x : x + 2, 2 : ny + 2, :]
        for j in range(2):
            col_out[i, j] = ext_ref[2 : nx + 2, y + j, :]
            edge = (0, ny + 2)[j]
            for k in range(2):
                edge_out[2 * i + j, 2 * k : 2 * k + 2] = ext_ref[x + k, edge : edge + 2, :]
    for copy in copies:
        copy.start()
    inner_rows(work, cells_x, cells_y)
    out_ref[...] = ext_ref[2 : nx + 2, 2 : ny + 2, :]
    for copy in copies:
        copy.wait()
    for i in range(2):
        x = (nx - 2, 0)[i]
        y = (ny - 2, 0)[i]
        out_ref[x : x + 2] = out_ref[x : x + 2] + row_in[i]
        for j in range(2):
            out_ref[:, y + j, :] = out_ref[:, y + j, :] + col_in[i, j]
            edge = (ny - 2, 0)[j]
            for k in range(2):
                out_ref[x + k, edge : edge + 2, :] = (
                    out_ref[x + k, edge : edge + 2, :] + edge_in[2 * i + j, 2 * k : 2 * k + 2]
                )


def gather_kernel(
    count_x, count_y, fraction_ref, base_ref, in_ref, out_ref, ext_ref, *scratch
):
    row_out, row_in, col_out, col_in, edge_out, edge_in, sent, here = scratch
    nx, ny, size = in_ref.shape
    cells_x, cells_y, slots = out_ref.shape

    def work(row, chosen):
        across = [spline_weights(fraction_ref[dim, row]) for dim in range(3)]
        for cell in chosen:
            window_x, window_y, depth = cell_tables(across, base_ref, row, cell, size)
            span = (pl.ds(row * CELL, REACH), pl.ds(cell * CELL, REACH), slice(None))
            window = ext_ref[span].reshape(REACH * REACH, size)
            value = dot3(halves(window), depth, NN).reshape(REACH, REACH, slots)
            value = jnp.sum(value * window_x[:, None, :], axis=0) * window_y
            out_ref[row, cell : cell + 1, :] = jnp.sum(value, axis=0, keepdims=True)

    for i in range(2):
        x = (0, nx - 2)[i]
        y = (0, ny - 2)[i]
        row_out[i] = in_ref[x : x + 2]
        for j in range(2):
            col_out[i, j] = in_ref[:, y + j, :]
            edge = (0, ny - 2)[j]
            for k in range(2):
                edge_out[2 * i + j, 2 * k : 2 * k + 2] = in_ref[x + k, edge : edge + 2, :]
    copies = neighbour_copies(count_x, count_y, *scratch)
    for copy in copies:
        copy.start()
    ext_ref[2 : nx + 2, 2 : ny + 2, :] = in_ref[...]
    inner_rows(work, cells_x, cells_y)
    for copy in copies:
        copy.wait()
    for i in range(2):
        x = (nx + 2, 0)[i]
        y = (ny + 2, 0)[i]
        ext_ref[x : x + 2, 2 : ny + 2, :] = row_in[i]
        for j in range(2):
            ext_ref[2 : nx + 2, y + j, :] = col_in[i, j]
            edge = (ny + 2, 0)[j]
            for k in range(2):
                ext_ref[x + k, edge : edge + 2, :] = edge_in[2 * i + j, 2 * k : 2 * k + 2]
    border_rows(work, cells_x, cells_y)


def halo_scratch(nx, ny, size):
    shapes = [(2, 2, ny, size)] * 2 + [(2, 2, nx, size)] * 2 + [(4, 4, size)] * 2
    shapes = [(nx + 4, ny + 4, size)] + shapes
    return [pltpu.VMEM(shape, jnp.float32) for shape in shapes] + [
        pltpu.SemaphoreType.DMA((8,)),
        pltpu.SemaphoreType.DMA((8,)),
    ]


def wave_tables(size, devices, scale):
    each = size // devices
    rows, weights = [], []
    points = np.arange(size)
    for device in range(devices):
        for plane in range(each // 2):
            wave = device * each + plane + (0 if device < devices // 2 else 1)
            angle = (wave * points % size) * (2.0 * math.pi / size)
            if wave == 0:
                rows += [np.ones(size), 1.0 - 2.0 * (points % 2)]
                weights += [1.0, 1.0]
            else:
                rows += [np.cos(angle), -np.sin(angle)]
                weights += [2.0, 2.0]
    forward = np.stack(rows)
    return forward, forward * (np.array(weights)[:, None] * scale)


def angles(first, second, size):
    return (first[:, None] * second[None, :] % size) * (2.0 * math.pi / size)


def per_device(cotangent, fraction, grid_base, cell_count, influence):
    cells_x, cells_y, slots = cotangent.shape
    full_x, full_y = influence.shape[1:]
    px_size = lax.axis_size("px")
    py_size = lax.axis_size("py")
    devices = px_size * py_size
    each = influence.shape[0]
    size = each * devices
    planes = each // 2
    local_x = cells_x * CELL
    local_y = cells_y * CELL
    pairs = local_x // 2
    lanes = 2 * local_y
    params = pltpu.CompilerParams(vmem_limit_bytes=VMEM_LIMIT)
    occupied = jnp.arange(slots, dtype=jnp.int32)[None, None, :] < cell_count[:, :, None]
    charge = jnp.where(occupied, cotangent, 0.0)

    def linked(number):
        return pltpu.CompilerParams(
            vmem_limit_bytes=VMEM_LIMIT, collective_id=number, has_side_effects=True
        )

    spread = pl.pallas_call(
        functools.partial(spread_kernel, px_size, py_size),
        out_shape=jax.ShapeDtypeStruct((local_x, local_y, size), jnp.float32),
        scratch_shapes=halo_scratch(local_x, local_y, size),
        compiler_params=linked(0),
        name="spread",
    )(charge, fraction, grid_base)

    forward_z, inverse_z = wave_tables(size, devices, 1.0 / (size * full_x * full_y))
    columns = pl.pallas_call(
        depth_forward_kernel,
        out_shape=jax.ShapeDtypeStruct((size * pairs, lanes), jnp.float32),
        compiler_params=params,
        name="depth_forward",
    )(spread, halves_np(forward_z))
    order = np.arange(full_x).reshape(full_x // 2, 2).T.reshape(-1)
    y_angles = angles(np.arange(full_y), np.arange(full_y), full_y)
    x_angles = angles(np.arange(full_x), order, full_x)
    right = np.concatenate([np.cos(y_angles), -np.sin(y_angles)], axis=1)
    back = np.concatenate([np.cos(y_angles), np.sin(y_angles)], axis=1)
    left = np.concatenate([np.cos(x_angles), -np.sin(x_angles)], axis=0)
    left_back = np.concatenate([np.cos(x_angles.T), np.sin(x_angles.T)], axis=0)
    chunks = (devices, planes, 2, pairs, lanes)
    landing = pltpu.VMEM((planes, devices, 2, pairs, lanes), jnp.float32)
    in_vmem = pl.BlockSpec(memory_space=pltpu.VMEM)
    returned = pl.pallas_call(
        functools.partial(exchange_kernel, px_size, py_size),
        in_specs=[in_vmem] * 6,
        out_specs=in_vmem,
        out_shape=jax.ShapeDtypeStruct(chunks, jnp.float32),
        scratch_shapes=[landing, landing, pltpu.VMEM((full_x, full_y), jnp.float32)]
        + [pltpu.SemaphoreType.DMA((planes,))] * 4
        + [pltpu.SemaphoreType.DMA] * 2,
        compiler_params=linked(1),
        name="exchange",
    )(
        columns.reshape(chunks),
        influence,
        halves_np(right),
        halves_np(back),
        halves_np(left),
        halves_np(left_back),
    ).reshape(size * pairs, lanes)
    potential = pl.pallas_call(
        depth_inverse_kernel,
        out_shape=jax.ShapeDtypeStruct((local_x, local_y, size), jnp.float32),
        compiler_params=params,
        name="depth_inverse",
    )(returned, halves_np(inverse_z))
    gradient = pl.pallas_call(
        functools.partial(gather_kernel, px_size, py_size),
        out_shape=jax.ShapeDtypeStruct(cotangent.shape, jnp.float32),
        scratch_shapes=halo_scratch(local_x, local_y, size),
        compiler_params=linked(2),
        name="gather",
    )(fraction, grid_base, potential)
    return jnp.where(occupied, gradient, 0.0)


def solution(mesh):
    placed = (
        P("px", "py", None),
        P(None, "px", "py", None),
        P(None, "px", "py", None),
        P("px", "py"),
        P(("px", "py"), None, None),
    )
    return jax.shard_map(
        per_device, mesh=mesh, in_specs=placed, out_specs=P("px", "py", None), check_vma=False
    )
```
